512 devices in a mesh: tp: 8 (over z_hi, x), dp: 64 (over y, z_lo, core).
Axes of the slice: x: 4, y: 4, z: 16 (z_hi: 2, z_lo: 8; z = z_hi * 8 + z_lo), core: 2. Of those that a mesh axis runs over, the one named last changes fastest.
Arguments:
- features: bfloat16 [8192, 1536], P('dp', 'tp'), may hold values from -2 to 2
- proj_weight: bfloat16 [1536, 1024], P('tp'), may hold values from -0.15625 to 0.15625
- text_embed: bfloat16 [8192, 1024], P(('tp', 'dp')), may hold values from -2 to 2
- log_scale: float32 [1], replicated, may hold values from 2 to 2.6
- logit_bias: float32 [1], replicated, may hold values from -7 to -5
Outputs:
- image_grad: bfloat16 [8192, 1536], P('dp', 'tp')
- weight_grad: bfloat16 [1536, 1024], P('tp')
- text_grad: bfloat16 [8192, 1024], P(('tp', 'dp'))
The draws below stay inside these ranges and needn't reach their ends.
All inputs are finite; a program needn't handle non-finite values.
Results may differ from the reference program's by a relative error of at most 0.0063.
Values may be sent and summed in bfloat16 or wider, within the bound.
No kernel may reach another device: no remote copies, remote signals or barrier semaphores. Data moves between devices by JAX's collectives and lax.ppermute only.
A program may use at most 64 MiB of HBM per device.

```python
import math
import jax
import jax.numpy as jnp
from jax import lax

FEAT = 1536
EMB = 1024
BATCH = 8192


def scaled_rows(sample, key_scale, row_count, largest):
    row_scales = jnp.exp(jax.random.uniform(key_scale, (row_count, 1), minval=0.0, maxval=math.log(largest)))
    return (0.03 * sample * row_scales).astype(jnp.float32)


def draw_features(key, part):
    key = jax.random.fold_in(key, 11)
    key_main, key_scale = jax.random.split(key, 2)
    sample = jnp.clip(jax.random.normal(key_main, (BATCH, FEAT)), -4.0, 4.0)
    return scaled_rows(sample, key_scale, BATCH, 10.0).astype(jnp.bfloat16)


def draw_text_embed(key, part):
    key = jax.random.fold_in(key, 23)
    key_main, key_scale = jax.random.split(key, 2)
    sample = jnp.clip(jax.random.normal(key_main, (BATCH, EMB)), -4.0, 4.0)
    return scaled_rows(sample, key_scale, BATCH, 10.0).astype(jnp.bfloat16)


def levels(stream_key, dims, shards, least, top_value):
    def one(dim, parts):
        steps = jax.random.uniform(jax.random.fold_in(jax.random.fold_in(stream_key, 6), dim), (parts,), jnp.float32, least / len(shards), top_value / len(shards))
        return jnp.repeat(jnp.exp(steps), dims[dim] // parts).reshape((-1,) + (1,) * (len(dims) - dim - 1))

    gain = one(*shards[0])
    for cut in shards[1:]:
        gain = gain * one(*cut)
    return gain


def noise(own_key, dims, width, bound, cuts=(), kind=jnp.bfloat16):
    drawn = jax.random.normal(own_key, dims, jnp.float32) * width
    if len(cuts) > 0:
        drawn = levels(own_key, dims, cuts, -0.22, 0.18) * drawn
    return jnp.clip(drawn, min=-bound, max=bound).astype(kind)


def setup_inputs(seed: int = 0) -> dict:
    keys = jax.random.split(jax.random.key(seed), 6)
    features = draw_features(jax.random.fold_in(keys[5], 71), 0)
    proj_weight = noise(keys[1], (FEAT, EMB), FEAT ** -0.5, 0.15625, ((0, 8),))
    text_embed = draw_text_embed(jax.random.fold_in(keys[5], 71), 0)
    log_scale = jnp.clip(jax.random.uniform(keys[3], (1,), jnp.float32, 2.0, 2.6), 2.0, 2.6)
    logit_bias = jnp.clip(jax.random.uniform(keys[4], (1,), jnp.float32, -7.0, -5.0), -7.0, -5.0)
    return dict(features=features, proj_weight=proj_weight, text_embed=text_embed, log_scale=log_scale, logit_bias=logit_bias)


def unit_backward(grad_unit, unit_value, inverse):
    along = lax.optimization_barrier(jnp.sum(unit_value * grad_unit, axis=1, keepdims=True))
    return inverse * (grad_unit - along * unit_value)

def reference(features, proj_weight, text_embed, log_scale, logit_bias):
    raw_embed = jnp.dot(features, proj_weight, preferred_element_type=jnp.float32)
    image_inverse = lax.rsqrt(lax.optimization_barrier(jnp.sum(raw_embed * raw_embed, axis=1, keepdims=True)) + 1e-06)
    unit_full = raw_embed * image_inverse
    image_unit = unit_full.astype(jnp.bfloat16)
    text_value = text_embed.astype(jnp.float32)
    text_inverse = lax.rsqrt(lax.optimization_barrier(jnp.sum(text_value * text_value, axis=1, keepdims=True)) + 1e-06)
    text_full = text_value * text_inverse
    text_unit = text_full.astype(jnp.bfloat16)
    temper = jnp.exp(log_scale[0])
    logit_shift = logit_bias[0]
    block_size = math.gcd(BATCH, 512)
    block_count = BATCH // block_size
    text_ids = jnp.arange(BATCH, dtype=jnp.int32)[None, :]

    def advance(accum, block_index):
        first_row = (block_index * block_size).astype(jnp.int32)
        row_block = lax.dynamic_slice_in_dim(image_unit, first_row, block_size, 0)
        logits = temper * jnp.dot(row_block, text_unit.T, preferred_element_type=jnp.float32) + logit_shift
        image_ids = first_row + jnp.arange(block_size, dtype=jnp.int32)[:, None]
        labels = jnp.where(image_ids == text_ids, 1.0, -1.0).astype(jnp.float32)
        coeffs = (-labels * jax.nn.sigmoid(-labels * logits) * temper).astype(jnp.bfloat16)
        grad_block = jnp.dot(coeffs, text_unit, preferred_element_type=jnp.float32)
        accum = accum + jnp.dot(coeffs.T, row_block, preferred_element_type=jnp.float32)
        return (accum, grad_block)
    text_unit_grad, grad_blocks = lax.scan(advance, jnp.zeros((BATCH, EMB), jnp.float32), jnp.arange(block_count, dtype=jnp.int32))
    unit_grad = grad_blocks.reshape(BATCH, EMB)
    embed_grad = unit_backward(unit_grad, unit_full, image_inverse).astype(jnp.bfloat16)
    image_grad = jnp.dot(embed_grad, proj_weight.T, preferred_element_type=jnp.float32).astype(jnp.bfloat16)
    weight_grad = jnp.dot(features.T, embed_grad, preferred_element_type=jnp.float32).astype(jnp.bfloat16)
    text_grad = unit_backward(text_unit_grad, text_full, text_inverse).astype(jnp.bfloat16)
    return (image_grad, weight_grad, text_grad)
```

```python
import jax
import jax.numpy as jnp
from jax import lax
from jax.sharding import Mesh, PartitionSpec as P

AXES = ("zh", "x", "y", "zl", "c")
BF = jnp.bfloat16
F32 = jnp.float32


def exchange(value, axes):
    return lax.all_to_all(value, axes, 0, 0, tiled=False)


def gather(value, axes):
    count = lax.axis_size(axes)
    return exchange(jnp.broadcast_to(value[None], (count,) + value.shape), axes)


def swap(value, axis):
    return lax.ppermute(value, axis, [(0, 1), (1, 0)])


def unit_backward(grad_unit, unit_value, inverse):
    along = jnp.sum(unit_value * grad_unit, axis=1, keepdims=True)
    return inverse * (grad_unit - along * unit_value)


def shards(features, proj_weight, text_embed, log_scale, logit_bias):
    zh, x, y, zl, c = (lax.axis_index(name) for name in AXES)
    nx, ny, nzl = (lax.axis_size(name) for name in ("x", "y", "zl"))
    emb = proj_weight.shape[1]
    block_rows = features.shape[0]
    own_rows = block_rows // nx
    text_rows = text_embed.shape[0]
    temper = jnp.exp(log_scale[0])
    logit_shift = logit_bias[0]

    partial_value = jnp.dot(features, proj_weight, preferred_element_type=F32).astype(BF)
    parts = exchange(partial_value.reshape(nx, own_rows, emb), "x")
    half_embed = jnp.sum(parts.astype(F32), axis=0)

    text_value = text_embed.astype(F32)
    text_inverse = lax.rsqrt(jnp.sum(text_value * text_value, axis=1, keepdims=True) + 1e-06)
    text_full = text_value * text_inverse
    text_unit = text_full.astype(BF)

    half_sent, text_unit = lax.optimization_barrier((half_embed.astype(BF), text_unit))
    other_half = swap(half_sent, "zh")
    text_line = gather(text_unit, "zl").reshape(nzl * text_rows, emb)
    raw_embed = half_embed + other_half.astype(F32)
    text_pair = swap(text_line, "c")
    text_block = jnp.concatenate([text_line, text_pair], axis=0)

    image_inverse = lax.rsqrt(jnp.sum(raw_embed * raw_embed, axis=1, keepdims=True) + 1e-06)
    unit_full = raw_embed * image_inverse
    image_unit = unit_full.astype(BF)
    image_block = gather(image_unit, ("y", "x")).reshape(ny * block_rows, emb)

    image_y = jnp.arange(ny, dtype=jnp.int32)[:, None]
    image_r = jnp.arange(block_rows, dtype=jnp.int32)[None, :]
    image_ids = (((image_y * nzl + zl) * 2 + c) * block_rows + image_r).reshape(-1, 1)
    text_c = jnp.stack([c, 1 - c]).astype(jnp.int32)[:, None, None]
    text_l = jnp.arange(nzl, dtype=jnp.int32)[None, :, None]
    text_r = jnp.arange(text_rows, dtype=jnp.int32)[None, None, :]
    text_group = (zh * nx + x) * ny + y
    text_ids = (((text_group * nzl + text_l) * 2 + text_c) * text_rows + text_r).reshape(1, -1)

    logits = (
        temper
        * lax.dot_general(
            image_block, text_block, (((1,), (1,)), ((), ())), preferred_element_type=F32
        )
        + logit_shift
    )
    labels = jnp.where(image_ids == text_ids, 1.0, -1.0).astype(F32)
    coeffs = (-labels * jax.nn.sigmoid(-labels * logits) * temper).astype(BF)

    unit_part = jnp.dot(coeffs, text_block, preferred_element_type=F32).astype(BF)
    unit_parts = exchange(unit_part.reshape(ny * nx, own_rows, emb), ("y", "x"))
    half_grad = jnp.sum(unit_parts.astype(F32), axis=0)

    text_part = lax.dot_general(
        coeffs, image_block, (((0,), (0,)), ((), ())), preferred_element_type=F32
    )
    line_rows = nzl * text_rows
    text_away = swap(text_part[line_rows:].astype(BF), "c")
    text_home = (text_part[:line_rows] + text_away.astype(F32)).astype(BF)

    grad_sent, text_home = lax.optimization_barrier((half_grad.astype(BF), text_home))
    other_grad = swap(grad_sent, "zh")
    text_parts = exchange(text_home.reshape(nzl, text_rows, emb), "zl")
    unit_grad = half_grad + other_grad.astype(F32)
    embed_rows = unit_backward(unit_grad, unit_full, image_inverse).astype(BF)
    embed_grad = gather(embed_rows, "x").reshape(block_rows, emb)

    weight_part = lax.dot_general(
        features, embed_grad, (((0,), (0,)), ((), ())), preferred_element_type=F32
    ).astype(BF)
    image_grad = lax.dot_general(
        embed_grad, proj_weight, (((1,), (1,)), ((), ())), preferred_element_type=F32
    ).astype(BF)
    pieces = ny * 2
    weight_rows = weight_part.shape[0] // pieces
    weight_parts = exchange(weight_part.reshape(pieces, weight_rows, emb), ("y", "c"))
    weight_sum = jnp.sum(weight_parts.astype(F32), axis=0).astype(BF)
    weight_line = gather(weight_sum, "zl")
    weight_own = jnp.sum(weight_line.astype(F32), axis=0).astype(BF)
    weight_grad = gather(weight_own, ("y", "c")).reshape(weight_part.shape)

    text_unit_grad = jnp.sum(text_parts.astype(F32), axis=0)
    text_grad = unit_backward(text_unit_grad, text_full, text_inverse).astype(BF)
    return (image_grad, weight_grad, text_grad)


def solution(mesh):
    fine = Mesh(mesh.devices.reshape(2, 4, 4, 8, 2), AXES)
    tp, dp = ("zh", "x"), ("y", "zl", "c")
    return jax.shard_map(
        shards,
        mesh=fine,
        in_specs=(P(dp, tp), P(tp, None), P(tp + dp, None), P(), P()),
        out_specs=(P(dp, tp), P(tp, None), P(tp + dp, None)),
        check_vma=False,
    )
```

```python
import jax
import jax.numpy as jnp
from jax import lax
from jax.sharding import Mesh, PartitionSpec as P

AXES = ("zh", "x", "y", "zl", "c")
BF = jnp.bfloat16
F32 = jnp.float32


def exchange(value, axes):
    return lax.all_to_all(value, axes, 0, 0, tiled=False)


def gather(value, axes):
    count = lax.axis_size(axes)
    return exchange(jnp.broadcast_to(value[None], (count,) + value.shape), axes)


def flip(value, axis, bit=1):
    return lax.ppermute(value, axis, [(i, i ^ bit) for i in range(lax.axis_size(axis))])


def unit_backward(grad_unit, unit_value, inverse):
    along = jnp.sum(unit_value * grad_unit, axis=1, keepdims=True)
    return inverse * (grad_unit - along * unit_value)


def shards(features, proj_weight, text_embed, log_scale, logit_bias):
    zh, x, y, zl, c = (lax.axis_index(name) for name in AXES)
    nx, ny, nzl = (lax.axis_size(name) for name in ("x", "y", "zl"))
    emb = proj_weight.shape[1]
    block_rows = features.shape[0]
    own_rows = block_rows // nx
    text_rows = text_embed.shape[0]
    temper = jnp.exp(log_scale[0])
    logit_shift = logit_bias[0]

    partial_value = jnp.dot(features, proj_weight, preferred_element_type=F32).astype(BF)
    parts = exchange(partial_value.reshape(nx, own_rows, emb), "x")
    half_embed = jnp.sum(parts.astype(F32), axis=0)

    text_value = text_embed.astype(F32)
    text_inverse = lax.rsqrt(jnp.sum(text_value * text_value, axis=1, keepdims=True) + 1e-06)
    text_full = text_value * text_inverse
    text_unit = text_full.astype(BF)

    half_sent, text_unit = lax.optimization_barrier((half_embed.astype(BF), text_unit))
    other_half = flip(half_sent, "zh")
    text_line = gather(text_unit, "zl").reshape(nzl * text_rows, emb)
    raw_embed = half_embed + other_half.astype(F32)
    text_pair = flip(text_line, "c")
    text_block = jnp.concatenate([text_line, text_pair], axis=0)

    image_inverse = lax.rsqrt(jnp.sum(raw_embed * raw_embed, axis=1, keepdims=True) + 1e-06)
    unit_full = raw_embed * image_inverse
    image_unit = unit_full.astype(BF)
    image_block = gather(image_unit, ("y", "x")).reshape(ny * block_rows, emb)

    image_y = jnp.arange(ny, dtype=jnp.int32)[:, None]
    image_r = jnp.arange(block_rows, dtype=jnp.int32)[None, :]
    image_ids = (((image_y * nzl + zl) * 2 + c) * block_rows + image_r).reshape(-1, 1)
    text_c = jnp.stack([c, 1 - c]).astype(jnp.int32)[:, None, None]
    text_l = jnp.arange(nzl, dtype=jnp.int32)[None, :, None]
    text_r = jnp.arange(text_rows, dtype=jnp.int32)[None, None, :]
    text_group = (zh * nx + x) * ny + y
    text_ids = (((text_group * nzl + text_l) * 2 + text_c) * text_rows + text_r).reshape(1, -1)

    logits = (
        temper
        * lax.dot_general(
            image_block, text_block, (((1,), (1,)), ((), ())), preferred_element_type=F32
        )
        + logit_shift
    )
    labels = jnp.where(image_ids == text_ids, 1.0, -1.0).astype(F32)
    coeffs = (-labels * jax.nn.sigmoid(-labels * logits) * temper).astype(BF)

    unit_part = jnp.dot(coeffs, text_block, preferred_element_type=F32).astype(BF)
    unit_parts = exchange(unit_part.reshape(ny * nx, own_rows, emb), ("y", "x"))

    text_part = lax.dot_general(
        coeffs, image_block, (((0,), (0,)), ((), ())), preferred_element_type=F32
    )
    line_rows = nzl * text_rows
    text_away = flip(text_part[line_rows:].astype(BF), "c")
    text_home = (text_part[:line_rows] + text_away.astype(F32)).astype(BF)

    unit_parts, text_home = lax.optimization_barrier((unit_parts, text_home))
    half_grad = jnp.sum(unit_parts.astype(F32), axis=0)
    other_grad = flip(half_grad.astype(BF), "zh")
    unit_grad = half_grad + other_grad.astype(F32)
    embed_rows = unit_backward(unit_grad, unit_full, image_inverse).astype(BF)
    embed_grad = gather(embed_rows, "x").reshape(block_rows, emb)

    weight_part = lax.dot_general(
        features, embed_grad, (((0,), (0,)), ((), ())), preferred_element_type=F32
    ).astype(BF)
    image_grad = lax.dot_general(
        embed_grad, proj_weight, (((1,), (1,)), ((), ())), preferred_element_type=F32
    ).astype(BF)
    pieces = ny * 2
    weight_rows = weight_part.shape[0] // pieces
    weight_parts = exchange(weight_part.reshape(pieces, weight_rows, emb), ("y", "c"))
    weight_sum = jnp.sum(weight_parts.astype(F32), axis=0).astype(BF)
    text_sum = text_home.astype(F32).reshape(2, 2, 2, text_rows, emb)
    for bit, depth in ((1, 2), (2, 1), (4, 0)):
        upper = (zl & bit) > 0
        first = lax.index_in_dim(text_sum, 0, depth, keepdims=False)
        second = lax.index_in_dim(text_sum, 1, depth, keepdims=False)
        away = jnp.where(upper, first, second).astype(BF)
        sent = jnp.concatenate([weight_sum, away.reshape(-1, emb)], axis=0)
        came = flip(sent, "zl", bit).astype(F32)
        weight_sum = (weight_sum.astype(F32) + came[:weight_rows]).astype(BF)
        text_sum = jnp.where(upper, second, first) + came[weight_rows:].reshape(away.shape)
    text_unit_grad = text_sum
    weight_grad = gather(weight_sum, ("y", "c")).reshape(weight_part.shape)

    text_grad = unit_backward(text_unit_grad, text_full, text_inverse).astype(BF)
    return (image_grad, weight_grad, text_grad)


def solution(mesh):
    fine = Mesh(mesh.devices.reshape(2, 4, 4, 8, 2), AXES)
    tp, dp = ("zh", "x"), ("y", "zl", "c")
    return jax.shard_map(
        shards,
        mesh=fine,
        in_specs=(P(dp, tp), P(tp, None), P(tp + dp, None), P(), P()),
        out_specs=(P(dp, tp), P(tp, None), P(tp + dp, None)),
        check_vma=False,
    )
```

```python
import jax
import jax.numpy as jnp
from jax import lax
from jax.sharding import Mesh, PartitionSpec as P

AXES = ("zh", "x", "y", "zq", "zp", "c")
SIZES = (2, 4, 4, 4, 2, 2)
BF = jnp.bfloat16
F32 = jnp.float32


def exchange(value, axes):
    return lax.all_to_all(value, axes, 0, 0, tiled=False)


def gather(value, axes):
    count = lax.axis_size(axes)
    return exchange(jnp.broadcast_to(value[None], (count,) + value.shape), axes)


def flip(value, axis):
    return lax.ppermute(value, axis, [(0, 1), (1, 0)])


def fold(value, axis):
    rows = value.shape[0] // 2
    return value[:rows] + flip(value[rows:].astype(BF), axis).astype(F32)


def unit_backward(grad_unit, unit_value, inverse):
    along = jnp.sum(unit_value * grad_unit, axis=1, keepdims=True)
    return inverse * (grad_unit - along * unit_value)


def shards(features, proj_weight, text_embed, log_scale, logit_bias):
    zh, x, y, zq, zp, c = (lax.axis_index(name) for name in AXES)
    nx, ny, nq = (lax.axis_size(name) for name in ("x", "y", "zq"))
    emb = proj_weight.shape[1]
    block_rows = features.shape[0]
    own_rows = block_rows // nx
    text_rows = text_embed.shape[0]
    column_rows = nq * text_rows
    temper = jnp.exp(log_scale[0])
    logit_shift = logit_bias[0]

    partial_value = jnp.dot(features, proj_weight, preferred_element_type=F32).astype(BF)
    parts = exchange(partial_value.reshape(nx, own_rows, emb), "x")
    half_embed = jnp.sum(parts.astype(F32), axis=0)

    text_value = text_embed.astype(F32)
    text_inverse = lax.rsqrt(jnp.sum(text_value * text_value, axis=1, keepdims=True) + 1e-06)
    text_full = text_value * text_inverse
    text_unit = text_full.astype(BF)

    half_sent, text_unit = lax.optimization_barrier((half_embed.astype(BF), text_unit))
    other_half = flip(half_sent, "zh")
    text_far = gather(text_unit, ("zh", "zq")).reshape(2, column_rows, emb)
    text_both = jnp.stack(
        [lax.dynamic_index_in_dim(text_far, i, axis=0, keepdims=False) for i in (zh, 1 - zh)]
    )[:, None]
    text_both = jnp.concatenate([text_both, flip(text_both, "zp")], axis=1)[:, None]
    text_both = jnp.concatenate([text_both, flip(text_both, "c")], axis=1)
    text_block = text_both.reshape(8 * column_rows, emb)

    raw_embed = half_embed + other_half.astype(F32)
    image_inverse = lax.rsqrt(jnp.sum(raw_embed * raw_embed, axis=1, keepdims=True) + 1e-06)
    unit_full = raw_embed * image_inverse
    image_unit = unit_full.astype(BF)
    image_block = gather(image_unit, ("y", "x")).reshape(ny * block_rows, emb)

    def ids(first, second, third, fourth):
        return (((first * nq + second) * 2 + third) * 2) + fourth

    image_y = jnp.arange(ny, dtype=jnp.int32)[:, None]
    image_r = jnp.arange(block_rows, dtype=jnp.int32)[None, :]
    image_ids = (ids(image_y, zq, zp, c) * block_rows + image_r).reshape(-1, 1)

    def near_far(place, axis):
        shape = [1] * 5
        shape[axis] = 2
        return jnp.stack([place, 1 - place]).astype(jnp.int32).reshape(shape)

    text_q = jnp.arange(nq, dtype=jnp.int32).reshape(1, 1, 1, -1, 1)
    text_r = jnp.arange(text_rows, dtype=jnp.int32).reshape(1, 1, 1, 1, -1)
    text_group = (near_far(zh, 0) * nx + x) * ny + y
    text_ids = ids(text_group, text_q, near_far(zp, 2), near_far(c, 1)) * text_rows + text_r
    text_ids = text_ids.reshape(1, -1)

    logits = (
        temper
        * lax.dot_general(
            image_block, text_block, (((1,), (1,)), ((), ())), preferred_element_type=F32
        )
        + logit_shift
    )
    labels = jnp.where(image_ids == text_ids, 1.0, -1.0).astype(F32)
    coeffs = (-labels * jax.nn.sigmoid(-labels * logits) * temper).astype(BF)

    unit_part = jnp.dot(coeffs, text_block, preferred_element_type=F32).astype(BF)
    unit_parts = exchange(unit_part.reshape(ny * nx, own_rows, emb), ("y", "x"))

    text_part = lax.dot_general(
        coeffs[:, : 4 * column_rows],
        image_block,
        (((0,), (0,)), ((), ())),
        preferred_element_type=F32,
    )
    text_home = fold(fold(text_part, "c"), "zp").astype(BF).reshape(nq, text_rows, emb)
    unit_parts, text_home = lax.optimization_barrier((unit_parts, text_home))
    unit_grad = jnp.sum(unit_parts.astype(F32), axis=0)
    embed_rows = unit_backward(unit_grad, unit_full, image_inverse).astype(BF)
    embed_grad = gather(embed_rows, "x").reshape(block_rows, emb)

    width = emb // 2
    weight_part = jnp.stack(
        [
            lax.dot_general(
                features, half, (((0,), (0,)), ((), ())), preferred_element_type=F32
            ).astype(BF)
            for half in (embed_grad[:, :width], embed_grad[:, width:])
        ]
    )
    image_grad = lax.dot_general(
        embed_grad, proj_weight, (((1,), (1,)), ((), ())), preferred_element_type=F32
    ).astype(BF)

    near = ("zp", "y", "c")
    weight_rows = features.shape[1] // (ny * 2)
    weight_parts = exchange(weight_part.reshape(ny * 4, weight_rows, width), near)
    weight_sum = jnp.sum(weight_parts.astype(F32), axis=0).astype(BF)
    line_sent = jnp.concatenate(
        [
            jnp.broadcast_to(weight_sum[None], (nq, weight_rows, width)),
            text_home[:, :, :width],
            text_home[:, :, width:],
        ],
        axis=1,
    )
    line_sum = jnp.sum(exchange(line_sent, "zq").astype(F32), axis=0)
    weight_own = line_sum[:weight_rows].astype(BF)
    weight_grad = gather(weight_own, near).reshape(2, features.shape[1], width)
    weight_grad = jnp.concatenate([weight_grad[0], weight_grad[1]], axis=1)

    text_sum = line_sum[weight_rows:]
    text_unit_grad = jnp.concatenate([text_sum[:text_rows], text_sum[text_rows:]], axis=1)
    text_grad = unit_backward(text_unit_grad, text_full, text_inverse).astype(BF)
    return (image_grad, weight_grad, text_grad)


def solution(mesh):
    fine = Mesh(mesh.devices.reshape(SIZES), AXES)
    tp, dp = ("zh", "x"), ("y", "zq", "zp", "c")
    return jax.shard_map(
        shards,
        mesh=fine,
        in_specs=(P(dp, tp), P(tp, None), P(tp + dp, None), P(), P()),
        out_specs=(P(dp, tp), P(tp, None), P(tp + dp, None)),
        check_vma=False,
    )
```

```python
import jax
import jax.numpy as jnp
from jax import lax
from jax.sharding import Mesh, PartitionSpec as P

AXES = ("zh", "x", "y", "zq", "zp", "c")
SIZES = (2, 4, 4, 4, 2, 2)
BF = jnp.bfloat16
F32 = jnp.float32


def exchange(value, axes):
    return lax.all_to_all(value, axes, 0, 0, tiled=False)


def gather(value, axes):
    count = lax.axis_size(axes)
    return exchange(jnp.broadcast_to(value[None], (count,) + value.shape), axes)


def flip(value, axis):
    return lax.ppermute(value, axis, [(0, 1), (1, 0)])


def fold(value, axis):
    rows = value.shape[0] // 2
    return value[:rows] + flip(value[rows:].astype(BF), axis).astype(F32)


def unit_backward(grad_unit, unit_value, inverse):
    along = jnp.sum(unit_value * grad_unit, axis=1, keepdims=True)
    return inverse * (grad_unit - along * unit_value)


def shards(features, proj_weight, text_embed, log_scale, logit_bias):
    zh, x, y, zq, zp, c = (lax.axis_index(name) for name in AXES)
    nx, ny, nq = (lax.axis_size(name) for name in ("x", "y", "zq"))
    emb = proj_weight.shape[1]
    block_rows = features.shape[0]
    own_rows = block_rows // nx
    text_rows = text_embed.shape[0]
    column_rows = nq * text_rows
    temper = jnp.exp(log_scale[0])
    logit_shift = logit_bias[0]

    partial_value = jnp.dot(features, proj_weight, preferred_element_type=F32).astype(BF)
    parts = partial_value.reshape(nx, own_rows, emb)
    half_embed = lax.dynamic_index_in_dim(parts, x, axis=0, keepdims=False).astype(F32)
    for step in (2, 1, 3):
        ring = [(i, (i + step) % nx) for i in range(nx)]
        away = lax.dynamic_index_in_dim(parts, (x + step) % nx, axis=0, keepdims=False)
        half_embed = half_embed + lax.ppermute(away, "x", ring).astype(F32)

    text_value = text_embed.astype(F32)
    text_inverse = lax.rsqrt(jnp.sum(text_value * text_value, axis=1, keepdims=True) + 1e-06)
    text_full = text_value * text_inverse
    text_unit = text_full.astype(BF)

    other_half = flip(half_embed.astype(BF), "zh")
    text_far = gather(text_unit, ("zh", "zq")).reshape(2, column_rows, emb)
    text_both = jnp.stack(
        [lax.dynamic_index_in_dim(text_far, i, axis=0, keepdims=False) for i in (zh, 1 - zh)]
    )[:, None]
    text_both = jnp.concatenate([text_both, flip(text_both, "zp")], axis=1)[:, None]
    text_both = jnp.concatenate([text_both, flip(text_both, "c")], axis=1)
    text_block = text_both.reshape(8 * column_rows, emb)

    raw_embed = half_embed + other_half.astype(F32)
    image_inverse = lax.rsqrt(jnp.sum(raw_embed * raw_embed, axis=1, keepdims=True) + 1e-06)
    unit_full = raw_embed * image_inverse
    image_unit = unit_full.astype(BF)
    image_block = gather(image_unit, ("y", "x")).reshape(ny * block_rows, emb)

    def ids(first, second, third, fourth):
        return (((first * nq + second) * 2 + third) * 2) + fourth

    image_y = jnp.arange(ny, dtype=jnp.int32)[:, None]
    image_r = jnp.arange(block_rows, dtype=jnp.int32)[None, :]
    image_ids = (ids(image_y, zq, zp, c) * block_rows + image_r).reshape(-1, 1)

    def near_far(place, axis):
        shape = [1] * 5
        shape[axis] = 2
        return jnp.stack([place, 1 - place]).astype(jnp.int32).reshape(shape)

    text_q = jnp.arange(nq, dtype=jnp.int32).reshape(1, 1, 1, -1, 1)
    text_r = jnp.arange(text_rows, dtype=jnp.int32).reshape(1, 1, 1, 1, -1)
    text_group = (near_far(zh, 0) * nx + x) * ny + y
    text_ids = ids(text_group, text_q, near_far(zp, 2), near_far(c, 1)) * text_rows + text_r
    text_ids = text_ids.reshape(1, -1)

    logits = (
        temper
        * lax.dot_general(
            image_block, text_block, (((1,), (1,)), ((), ())), preferred_element_type=F32
        )
        + logit_shift
    )
    labels = jnp.where(image_ids == text_ids, 1.0, -1.0).astype(F32)
    coeffs = (-labels * jax.nn.sigmoid(-labels * logits) * temper).astype(BF)

    unit_part = jnp.dot(coeffs, text_block, preferred_element_type=F32).astype(BF)
    unit_parts = exchange(unit_part.reshape(ny * nx, own_rows, emb), ("y", "x"))

    text_part = lax.dot_general(
        coeffs[:, : 4 * column_rows],
        image_block,
        (((0,), (0,)), ((), ())),
        preferred_element_type=F32,
    )
    text_home = fold(fold(text_part, "c"), "zp").astype(BF).reshape(nq, text_rows, emb)
    unit_parts, text_home = lax.optimization_barrier((unit_parts, text_home))
    unit_grad = jnp.sum(unit_parts.astype(F32), axis=0)
    embed_rows = unit_backward(unit_grad, unit_full, image_inverse).astype(BF)
    embed_grad = gather(embed_rows, "x").reshape(block_rows, emb)

    width = emb // 2
    weight_part = jnp.stack(
        [
            lax.dot_general(
                features, half, (((0,), (0,)), ((), ())), preferred_element_type=F32
            ).astype(BF)
            for half in (embed_grad[:, :width], embed_grad[:, width:])
        ]
    )
    image_grad = lax.dot_general(
        embed_grad, proj_weight, (((1,), (1,)), ((), ())), preferred_element_type=F32
    ).astype(BF)

    near = ("zp", "y", "c")
    weight_rows = features.shape[1] // (ny * 2)
    weight_parts = exchange(weight_part.reshape(ny * 4, weight_rows, width), near)
    weight_sum = jnp.sum(weight_parts.astype(F32), axis=0).astype(BF)
    line_sent = jnp.concatenate(
        [
            jnp.broadcast_to(weight_sum[None], (nq, weight_rows, width)),
            text_home[:, :, :width],
            text_home[:, :, width:],
        ],
        axis=1,
    )
    line_sum = jnp.sum(exchange(line_sent, "zq").astype(F32), axis=0)
    weight_own = line_sum[:weight_rows].astype(BF)
    weight_grad = gather(weight_own, near).reshape(2, features.shape[1], width)
    weight_grad = jnp.concatenate([weight_grad[0], weight_grad[1]], axis=1)

    text_sum = line_sum[weight_rows:]
    text_unit_grad = jnp.concatenate([text_sum[:text_rows], text_sum[text_rows:]], axis=1)
    text_grad = unit_backward(text_unit_grad, text_full, text_inverse).astype(BF)
    return (image_grad, weight_grad, text_grad)


def solution(mesh):
    fine = Mesh(mesh.devices.reshape(SIZES), AXES)
    tp, dp = ("zh", "x"), ("y", "zq", "zp", "c")
    return jax.shard_map(
        shards,
        mesh=fine,
        in_specs=(P(dp, tp), P(tp, None), P(tp + dp, None), P(), P()),
        out_specs=(P(dp, tp), P(tp, None), P(tp + dp, None)),
        check_vma=False,
    )
```

```python
import jax
import jax.numpy as jnp
from jax import lax
from jax.sharding import Mesh, PartitionSpec as P

AXES = ("zh", "x", "y", "zq", "zp", "c")
SIZES = (2, 4, 4, 4, 2, 2)
BF = jnp.bfloat16
F32 = jnp.float32


def exchange(value, axes):
    return lax.all_to_all(value, axes, 0, 0, tiled=False)


def gather(value, axes):
    count = lax.axis_size(axes)
    return exchange(jnp.broadcast_to(value[None], (count,) + value.shape), axes)


def flip(value, axis):
    return lax.ppermute(value, axis, [(0, 1), (1, 0)])


def fold(value, axis):
    rows = value.shape[0] // 2
    return value[:rows] + flip(value[rows:].astype(BF), axis).astype(F32)


def unit_backward(grad_unit, unit_value, inverse):
    along = jnp.sum(unit_value * grad_unit, axis=1, keepdims=True)
    return inverse * (grad_unit - along * unit_value)


def shards(features, proj_weight, text_embed, log_scale, logit_bias):
    zh, x, y, zq, zp, c = (lax.axis_index(name) for name in AXES)
    nx, ny, nq = (lax.axis_size(name) for name in ("x", "y", "zq"))
    emb = proj_weight.shape[1]
    block_rows = features.shape[0]
    own_rows = block_rows // nx
    text_rows = text_embed.shape[0]
    column_rows = nq * text_rows
    temper = jnp.exp(log_scale[0])
    logit_shift = logit_bias[0]

    partial_value = jnp.dot(features, proj_weight, preferred_element_type=F32).astype(BF)
    parts = partial_value.reshape(nx, own_rows, emb)
    half_embed = lax.dynamic_index_in_dim(parts, x, axis=0, keepdims=False).astype(F32)
    for bit in (2, 1, 3):
        pairs = [(i, i ^ bit) for i in range(nx)]
        away = lax.dynamic_index_in_dim(parts, x ^ bit, axis=0, keepdims=False)
        half_embed = half_embed + lax.ppermute(away, "x", pairs).astype(F32)

    text_value = text_embed.astype(F32)
    text_inverse = lax.rsqrt(jnp.sum(text_value * text_value, axis=1, keepdims=True) + 1e-06)
    text_full = text_value * text_inverse
    text_unit = text_full.astype(BF)

    other_half = flip(half_embed.astype(BF), "zh")
    text_far = gather(text_unit, ("zh", "zq")).reshape(2, column_rows, emb)
    text_both = jnp.stack(
        [lax.dynamic_index_in_dim(text_far, i, axis=0, keepdims=False) for i in (zh, 1 - zh)]
    )[:, None]
    text_both = jnp.concatenate([text_both, flip(text_both, "zp")], axis=1)[:, None]
    text_both = jnp.concatenate([text_both, flip(text_both, "c")], axis=1)
    text_block = text_both.reshape(8 * column_rows, emb)

    raw_embed = half_embed + other_half.astype(F32)
    image_inverse = lax.rsqrt(jnp.sum(raw_embed * raw_embed, axis=1, keepdims=True) + 1e-06)
    unit_full = raw_embed * image_inverse
    image_unit = unit_full.astype(BF)
    image_block = gather(image_unit, ("y", "x")).reshape(ny * block_rows, emb)

    def ids(first, second, third, fourth):
        return (((first * nq + second) * 2 + third) * 2) + fourth

    image_y = jnp.arange(ny, dtype=jnp.int32)[:, None]
    image_r = jnp.arange(block_rows, dtype=jnp.int32)[None, :]
    image_ids = (ids(image_y, zq, zp, c) * block_rows + image_r).reshape(-1, 1)

    def near_far(place, axis):
        shape = [1] * 5
        shape[axis] = 2
        return jnp.stack([place, 1 - place]).astype(jnp.int32).reshape(shape)

    text_q = jnp.arange(nq, dtype=jnp.int32).reshape(1, 1, 1, -1, 1)
    text_r = jnp.arange(text_rows, dtype=jnp.int32).reshape(1, 1, 1, 1, -1)
    text_group = (near_far(zh, 0) * nx + x) * ny + y
    text_ids = ids(text_group, text_q, near_far(zp, 2), near_far(c, 1)) * text_rows + text_r
    text_ids = text_ids.reshape(1, -1)

    logits = (
        temper
        * lax.dot_general(
            image_block, text_block, (((1,), (1,)), ((), ())), preferred_element_type=F32
        )
        + logit_shift
    )
    labels = jnp.where(image_ids == text_ids, 1.0, -1.0).astype(F32)
    coeffs = (-labels * jax.nn.sigmoid(-labels * logits) * temper).astype(BF)

    unit_part = jnp.dot(coeffs, text_block, preferred_element_type=F32).astype(BF)
    unit_parts = exchange(unit_part.reshape(ny * nx, own_rows, emb), ("y", "x"))

    text_part = lax.dot_general(
        coeffs[:, : 4 * column_rows],
        image_block,
        (((0,), (0,)), ((), ())),
        preferred_element_type=F32,
    )
    text_home = fold(fold(text_part, "c"), "zp").astype(BF).reshape(nq, text_rows, emb)
    unit_parts, text_home = lax.optimization_barrier((unit_parts, text_home))
    unit_grad = jnp.sum(unit_parts.astype(F32), axis=0)
    embed_rows = unit_backward(unit_grad, unit_full, image_inverse).astype(BF)
    embed_grad = gather(embed_rows, "x").reshape(block_rows, emb)

    width = emb // 2
    weight_part = jnp.stack(
        [
            lax.dot_general(
                features, half, (((0,), (0,)), ((), ())), preferred_element_type=F32
            ).astype(BF)
            for half in (embed_grad[:, :width], embed_grad[:, width:])
        ]
    )
    image_grad = lax.dot_general(
        embed_grad, proj_weight, (((1,), (1,)), ((), ())), preferred_element_type=F32
    ).astype(BF)

    near = ("zp", "y", "c")
    weight_rows = features.shape[1] // (ny * 2)
    weight_parts = exchange(weight_part.reshape(ny * 4, weight_rows, width), near)
    weight_sum = jnp.sum(weight_parts.astype(F32), axis=0).astype(BF)
    line_sent = jnp.concatenate(
        [
            jnp.broadcast_to(weight_sum[None], (nq, weight_rows, width)),
            text_home[:, :, :width],
            text_home[:, :, width:],
        ],
        axis=1,
    )
    line_sum = jnp.sum(exchange(line_sent, "zq").astype(F32), axis=0)
    weight_own = line_sum[:weight_rows].astype(BF)
    weight_grad = gather(weight_own, near).reshape(2, features.shape[1], width)
    weight_grad = jnp.concatenate([weight_grad[0], weight_grad[1]], axis=1)

    text_sum = line_sum[weight_rows:]
    text_unit_grad = jnp.concatenate([text_sum[:text_rows], text_sum[text_rows:]], axis=1)
    text_grad = unit_backward(text_unit_grad, text_full, text_inverse).astype(BF)
    return (image_grad, weight_grad, text_grad)


def solution(mesh):
    fine = Mesh(mesh.devices.reshape(SIZES), AXES)
    tp, dp = ("zh", "x"), ("y", "zq", "zp", "c")
    return jax.shard_map(
        shards,
        mesh=fine,
        in_specs=(P(dp, tp), P(tp, None), P(tp + dp, None), P(), P()),
        out_specs=(P(dp, tp), P(tp, None), P(tp + dp, None)),
        check_vma=False,
    )
```

```python
import jax
import jax.numpy as jnp
from jax import lax
from jax.sharding import Mesh, PartitionSpec as P

AXES = ("zh", "x", "y", "zq", "zp", "c")
SIZES = (2, 4, 4, 4, 2, 2)
BF = jnp.bfloat16
F32 = jnp.float32


def exchange(value, axes):
    return lax.all_to_all(value, axes, 0, 0, tiled=False)


def gather(value, axes):
    count = lax.axis_size(axes)
    return exchange(jnp.broadcast_to(value[None], (count,) + value.shape), axes)


def flip(value, axis):
    return lax.ppermute(value, axis, [(0, 1), (1, 0)])


def fold(value, axis):
    rows = value.shape[0] // 2
    return value[:rows] + flip(value[rows:].astype(BF), axis).astype(F32)


def unit_backward(grad_unit, unit_value, inverse):
    along = jnp.sum(unit_value * grad_unit, axis=1, keepdims=True)
    return inverse * (grad_unit - along * unit_value)


def shards(features, proj_weight, text_embed, log_scale, logit_bias):
    zh, x, y, zq, zp, c = (lax.axis_index(name) for name in AXES)
    nx, ny, nq = (lax.axis_size(name) for name in ("x", "y", "zq"))
    emb = proj_weight.shape[1]
    block_rows = features.shape[0]
    own_rows = block_rows // nx
    text_rows = text_embed.shape[0]
    column_rows = nq * text_rows
    temper = jnp.exp(log_scale[0])
    logit_shift = logit_bias[0]

    partial_value = jnp.dot(features, proj_weight, preferred_element_type=F32).astype(BF)
    parts = partial_value.reshape(nx, own_rows, emb)
    half_embed = lax.dynamic_index_in_dim(parts, x, axis=0, keepdims=False).astype(F32)
    for step in (2, 1, 3):
        ring = [(i, (i + step) % nx) for i in range(nx)]
        away = lax.dynamic_index_in_dim(parts, (x + step) % nx, axis=0, keepdims=False)
        half_embed = half_embed + lax.ppermute(away, "x", ring).astype(F32)

    text_value = text_embed.astype(F32)
    text_inverse = lax.rsqrt(jnp.sum(text_value * text_value, axis=1, keepdims=True) + 1e-06)
    text_full = text_value * text_inverse
    text_unit = text_full.astype(BF)

    other_half = flip(half_embed.astype(BF), "zh")
    text_far = gather(text_unit, ("zh", "zq")).reshape(2, column_rows, emb)
    text_both = jnp.stack(
        [lax.dynamic_index_in_dim(text_far, i, axis=0, keepdims=False) for i in (zh, 1 - zh)]
    )[:, None]
    text_both = jnp.concatenate([text_both, flip(text_both, "zp")], axis=1)[:, None]
    text_both = jnp.concatenate([text_both, flip(text_both, "c")], axis=1)
    text_block = text_both.reshape(8 * column_rows, emb)

    raw_embed = half_embed + other_half.astype(F32)
    image_inverse = lax.rsqrt(jnp.sum(raw_embed * raw_embed, axis=1, keepdims=True) + 1e-06)
    unit_full = raw_embed * image_inverse
    image_unit = unit_full.astype(BF)
    image_block = gather(image_unit, ("y", "x")).reshape(ny * block_rows, emb)

    def ids(first, second, third, fourth):
        return (((first * nq + second) * 2 + third) * 2) + fourth

    image_y = jnp.arange(ny, dtype=jnp.int32)[:, None]
    image_r = jnp.arange(block_rows, dtype=jnp.int32)[None, :]
    image_ids = (ids(image_y, zq, zp, c) * block_rows + image_r).reshape(-1, 1)

    def near_far(place, axis):
        shape = [1] * 5
        shape[axis] = 2
        return jnp.stack([place, 1 - place]).astype(jnp.int32).reshape(shape)

    text_q = jnp.arange(nq, dtype=jnp.int32).reshape(1, 1, 1, -1, 1)
    text_r = jnp.arange(text_rows, dtype=jnp.int32).reshape(1, 1, 1, 1, -1)
    text_group = (near_far(zh, 0) * nx + x) * ny + y
    text_ids = ids(text_group, text_q, near_far(zp, 2), near_far(c, 1)) * text_rows + text_r
    text_ids = text_ids.reshape(1, -1)

    logits = (
        temper
        * lax.dot_general(
            image_block, text_block, (((1,), (1,)), ((), ())), preferred_element_type=F32
        )
        + logit_shift
    )
    labels = jnp.where(image_ids == text_ids, 1.0, -1.0).astype(F32)
    coeffs = (-labels * jax.nn.sigmoid(-labels * logits) * temper).astype(BF)

    unit_part = jnp.dot(coeffs, text_block, preferred_element_type=F32).astype(BF)
    unit_parts = exchange(unit_part.reshape(ny * nx, own_rows, emb), ("y", "x"))

    text_part = lax.dot_general(
        coeffs[:, : 4 * column_rows],
        image_block,
        (((0,), (0,)), ((), ())),
        preferred_element_type=F32,
    )
    text_home = fold(fold(text_part, "c"), "zp").astype(BF).reshape(nq, text_rows, emb)
    unit_parts, text_home = lax.optimization_barrier((unit_parts, text_home))
    unit_grad = jnp.sum(unit_parts.astype(F32), axis=0)
    embed_rows = unit_backward(unit_grad, unit_full, image_inverse).astype(BF)
    embed_grad = gather(embed_rows, "x").reshape(block_rows, emb)

    weight_part = lax.dot_general(
        features, embed_grad, (((0,), (0,)), ((), ())), preferred_element_type=F32
    ).astype(BF)
    image_grad = lax.dot_general(
        embed_grad, proj_weight, (((1,), (1,)), ((), ())), preferred_element_type=F32
    ).astype(BF)

    near = ("zp", "y", "c")
    weight_rows = features.shape[1] // (ny * 4)
    weight_parts = exchange(weight_part.reshape(ny * 4, weight_rows, emb), near)
    weight_sum = jnp.sum(weight_parts.astype(F32), axis=0).astype(BF)
    line_sent = jnp.concatenate(
        [text_home, jnp.broadcast_to(weight_sum[None], (nq,) + weight_sum.shape)], axis=1
    )
    line_sum = jnp.sum(exchange(line_sent, "zq").astype(F32), axis=0)
    weight_own = line_sum[text_rows:].astype(BF)
    weight_grad = gather(weight_own, near).reshape(weight_part.shape)

    text_unit_grad = line_sum[:text_rows]
    text_grad = unit_backward(text_unit_grad, text_full, text_inverse).astype(BF)
    return (image_grad, weight_grad, text_grad)


def solution(mesh):
    fine = Mesh(mesh.devices.reshape(SIZES), AXES)
    tp, dp = ("zh", "x"), ("y", "zq", "zp", "c")
    return jax.shard_map(
        shards,
        mesh=fine,
        in_specs=(P(dp, tp), P(tp, None), P(tp + dp, None), P(), P()),
        out_specs=(P(dp, tp), P(tp, None), P(tp + dp, None)),
        check_vma=False,
    )
```
